128 devices in a mesh: blk: 16 (over y, x_lo, core), band: 8 (over z, x_hi).
Axes of the slice: x: 4 (x_hi: 2, x_lo: 2; x = x_hi * 2 + x_lo), y: 4, z: 4, core: 2. Of those that a mesh axis runs over, the one named last changes fastest.
Arguments:
- object_band: bfloat16 [2, 2048, 6144], P(None, 'band', 'blk'), may hold values from -6 to 6
- probe: float32 [2, 256, 256], replicated, may hold values from -6 to 6
- amplitudes: bfloat16 [16, 8, 16, 4, 256, 256], P('blk', 'band'), may hold values from 0.099609375 to 4
- row_offsets: int32 [16, 8, 16, 4], P('blk', 'band'), may hold values from 0 to 255
- col_offsets: int32 [16, 8, 16, 4], P('blk', 'band'), may hold values from 0 to 128
- counts: int32 [16, 8, 16], P('blk', 'band'), may hold values from 1 to 4, as said below
Outputs:
- new_object: float32 [2, 2048, 6144], P(None, 'band', 'blk')
- probe_grad: float32 [2, 256, 256], replicated
The draws below stay inside these ranges and needn't reach their ends.
Inputs may be any that keep to these rules, and one draw needn't show every extreme that they name: `counts`: groups differ in load; some count equals 4.
All inputs are finite; a program needn't handle non-finite values.
Results may differ from the reference program's by a relative error of at most 0.0025.
The reference program's roundings to bfloat16 on the way (of `psi`, `half`, `difference` and `back`) count: a program that leaves them out, or rounds other values in their place, can miss the bound.
Values may be sent and summed in bfloat16 or wider, within the bound.
No kernel may reach another device: no remote copies, remote signals or barrier semaphores. Data moves between devices by JAX's collectives and lax.ppermute only.
A program may use at most 128 MiB of HBM per device.

```python
import math
import jax
import jax.numpy as jnp
from jax import lax

WIN = 256
ROWS_DEV = 256
TILE_W = 384
SLOTS = 4
ROWS = 2048
COLS = 6144
N_BLK = 16
N_BAND = 8


def draw_counts(key, part):
    key = jax.random.fold_in(key, 7)
    first, second, third = jax.random.split(key, 3)
    level = jax.random.randint(first, (N_BLK, 1, 1), 1, 4)
    limit = jnp.maximum(1, (SLOTS * level + 2) // 3)
    drawn = jax.random.randint(second, (N_BLK, N_BAND, N_BLK), 1, limit + 1)
    spot = jax.random.randint(third, (), 0, N_BLK * N_BAND * N_BLK)
    flat = jnp.arange(N_BLK * N_BAND * N_BLK, dtype=jnp.int32).reshape(N_BLK, N_BAND, N_BLK)
    return jnp.where(flat == spot, SLOTS, drawn).astype(jnp.int32)


def set_ends(values, rng, low, largest):
    longest = values.shape.index(max(values.shape))
    spots = []
    for shift in (0, 1):
        where = [jax.random.randint(jax.random.fold_in(rng, axis), (), 0, length) for axis, length in enumerate(values.shape)]
        where[longest] = (where[longest] + shift) % values.shape[longest]
        spots.append(tuple(where))
    return values.at[spots[0]].set(low).at[spots[1]].set(largest)


def block_levels(stream_key, extent, pieces, low, top_value):
    gain, own = 1.0, jax.random.fold_in(stream_key, 6)
    for position, blocks in pieces:
        steps = jnp.exp(jax.random.uniform(jax.random.fold_in(own, position), (blocks,), jnp.float32, low / len(pieces), top_value / len(pieces)))
        gain = gain * jnp.repeat(steps, extent[position] // blocks).reshape([-1 if axis == position else 1 for axis in range(len(extent))])
    return gain


def gaussian(key, shape, scale, most, shards=(), kind=jnp.bfloat16):
    factor_of = block_levels(key, shape, shards, -0.22, 0.18) if shards else 1.0
    values = jax.random.normal(key, shape, jnp.float32) * scale * factor_of
    return jnp.minimum(jnp.maximum(values, -most), most).astype(kind)


def setup_inputs(seed: int = 0) -> dict:
    streams_of = jax.random.split(jax.random.key(seed), 7)
    return {
        "object_band": gaussian(streams_of[0], (2, ROWS, COLS), 0.7, 6.0, ((1, 8), (2, 16))),
        "probe": gaussian(streams_of[1], (2, WIN, WIN), 1.0, 6.0, (), jnp.float32),
        "amplitudes": jnp.clip(jnp.exp(math.log(4.0) - 3.6927934 * jax.random.uniform(streams_of[2], (N_BLK, N_BAND, N_BLK, SLOTS, WIN, WIN), jnp.float32) ** block_levels(streams_of[2], (N_BLK, N_BAND, N_BLK, SLOTS, WIN, WIN), ((0, 16), (1, 8)), -0.2, 0.2)), 0.099609375, 4.0).astype(jnp.bfloat16),
        "row_offsets": set_ends(jax.random.randint(streams_of[3], (N_BLK, N_BAND, N_BLK, SLOTS), 0, ROWS_DEV), jax.random.fold_in(streams_of[3], 1), 0, ROWS_DEV - 1).astype(jnp.int32),
        "col_offsets": set_ends(jax.random.randint(streams_of[4], (N_BLK, N_BAND, N_BLK, SLOTS), 0, TILE_W - WIN + 1), jax.random.fold_in(streams_of[4], 1), 0, TILE_W - WIN).astype(jnp.int32),
        "counts": draw_counts(jax.random.fold_in(streams_of[6], 71), 0),
    }


object_rate = 0.5
modulus_soft = 0.5

def dft_tables(size):
    index_line = jnp.arange(size, dtype=jnp.int32)
    product = index_line[:, None] * index_line[None, :] % size
    angle = product.astype(jnp.float32) * (2.0 * math.pi / size)
    factor = 1.0 / math.sqrt(size)
    cosine = jnp.cos(angle) * factor
    sine = jnp.sin(angle) * factor
    left_fwd = jnp.concatenate([jnp.concatenate([cosine, sine], 1), jnp.concatenate([-sine, cosine], 1)], 0).astype(jnp.bfloat16)
    right_fwd = jnp.concatenate([jnp.concatenate([cosine, -sine], 1), jnp.concatenate([sine, cosine], 1)], 0).astype(jnp.bfloat16)
    left_inv = jnp.concatenate([jnp.concatenate([cosine, -sine], 1), jnp.concatenate([sine, cosine], 1)], 0).astype(jnp.bfloat16)
    right_inv = jnp.concatenate([jnp.concatenate([cosine, sine], 1), jnp.concatenate([-sine, cosine], 1)], 0).astype(jnp.bfloat16)
    return (left_fwd, right_fwd, left_inv, right_inv)

def update_terms(window_cells, probe, amplitude, tables):
    left_fwd, right_fwd, left_inv, right_inv = tables
    size = probe.shape[1]
    obj_re = window_cells[0].astype(jnp.float32)
    obj_im = window_cells[1].astype(jnp.float32)
    probe_re = probe[0]
    probe_im = probe[1]
    psi = jnp.concatenate([probe_re * obj_re - probe_im * obj_im, probe_re * obj_im + probe_im * obj_re], 0).astype(jnp.bfloat16)
    half = jnp.dot(left_fwd, psi, preferred_element_type=jnp.float32).astype(jnp.bfloat16)
    spectrum = jnp.dot(jnp.concatenate([half[:size], half[size:]], 1), right_fwd, preferred_element_type=jnp.float32)
    spec_re = spectrum[:, :size]
    spec_im = spectrum[:, size:]
    factor = amplitude.astype(jnp.float32) / jnp.sqrt(spec_re * spec_re + spec_im * spec_im + modulus_soft) - 1.0
    difference = jnp.concatenate([spec_re * factor, spec_im * factor], 0).astype(jnp.bfloat16)
    back = jnp.dot(left_inv, difference, preferred_element_type=jnp.float32).astype(jnp.bfloat16)
    change = jnp.dot(jnp.concatenate([back[:size], back[size:]], 1), right_inv, preferred_element_type=jnp.float32)
    chg_re = change[:, :size]
    chg_im = change[:, size:]
    object_part = jnp.stack([probe_re * chg_re + probe_im * chg_im, probe_re * chg_im - probe_im * chg_re])
    probe_part = jnp.stack([obj_re * chg_re + obj_im * chg_im, obj_re * chg_im - obj_im * chg_re])
    return (object_part, probe_part)

def reference(object_band, probe, amplitudes, row_offsets, col_offsets, counts):
    tables = dft_tables(WIN)
    padded = jnp.concatenate([object_band, jnp.zeros((2, WIN, COLS), object_band.dtype)], 1)
    totals = jnp.zeros((2, ROWS + WIN, COLS), jnp.float32)
    probe_terms = jnp.zeros((2, WIN, WIN), jnp.float32)
    total_slots = N_BLK * N_BAND * N_BLK * SLOTS

    def visit(carry, flat_index):
        slot = flat_index % SLOTS
        tile = flat_index // SLOTS % N_BLK
        band_row = flat_index // (SLOTS * N_BLK) % N_BAND
        group = flat_index // (SLOTS * N_BLK * N_BAND)
        live = slot < counts[group, band_row, tile]

        def work(inner):
            sums, grads = inner
            zero = jnp.int32(0)
            row_start = (band_row * ROWS_DEV + row_offsets[group, band_row, tile, slot]).astype(jnp.int32)
            col_start = (tile * TILE_W + col_offsets[group, band_row, tile, slot]).astype(jnp.int32)
            window_cells = lax.dynamic_slice(padded, (zero, row_start, col_start), (2, WIN, WIN))
            object_part, probe_part = update_terms(window_cells, probe, amplitudes[group, band_row, tile, slot], tables)
            current = lax.dynamic_slice(sums, (zero, row_start, col_start), (2, WIN, WIN))
            sums = lax.dynamic_update_slice(sums, current + object_part, (zero, row_start, col_start))
            return (sums, grads + probe_part)

        def skip(inner):
            return inner
        return (lax.cond(live, work, skip, carry), None)
    (totals, probe_terms), unused = lax.scan(visit, (totals, probe_terms), jnp.arange(total_slots, dtype=jnp.int32))
    power = jnp.sum(probe * probe) / (WIN * WIN)
    new_object = object_band.astype(jnp.float32) + object_rate * totals[:, :ROWS] / (power + 1e-06)
    return (new_object, probe_terms / N_BLK)
```

```python
import functools
import math

import jax
import jax.numpy as jnp
from jax import lax
from jax.experimental import pallas as pl
from jax.experimental.pallas import tpu as pltpu
from jax.sharding import PartitionSpec as P

object_rate = 0.5
modulus_soft = 0.5
LANES = 128


def dft_tables(size):
    index_line = jnp.arange(size, dtype=jnp.int32)
    product = index_line[:, None] * index_line[None, :] % size
    angle = product.astype(jnp.float32) * (2.0 * math.pi / size)
    factor = 1.0 / math.sqrt(size)
    cosine = jnp.cos(angle) * factor
    sine = jnp.sin(angle) * factor
    plus = jnp.concatenate(
        [jnp.concatenate([cosine, sine], 1), jnp.concatenate([-sine, cosine], 1)], 0
    ).astype(jnp.bfloat16)
    minus = jnp.concatenate(
        [jnp.concatenate([cosine, -sine], 1), jnp.concatenate([sine, cosine], 1)], 0
    ).astype(jnp.bfloat16)
    return plus, minus


def position_kernel(plan, metas, sources, held, fresh_sums, fresh_grads, group_ref, *refs):
    pairs, first, many = plan
    meta = refs[:metas]
    amps = refs[metas : metas + sources]
    refs = refs[metas + sources :]
    mains, rims = refs[:held], refs[held : 2 * held]
    refs = refs[2 * held :]
    probe, plus, minus = refs[:3]
    rest = refs[3 + (not fresh_sums) + (not fresh_grads) :]
    sums, grads, cells, obj, diff, amp, live, arrived = rest
    size = probe.shape[1]
    across = size // LANES
    slots = meta[0].shape[1] // 2
    group = group_ref[0]

    count = jnp.int32(0)
    for origin, source, meta_row, unit_row, tile in pairs(group):
        for slot in range(first, first + many):
            live[count, 0] = jnp.int32(source)
            live[count, 1] = (unit_row * many + (slot - first)) * size
            live[count, 2] = jnp.int32(0)
            live[count, 3] = tile
            live[count, 4] = meta[origin][meta_row, slot]
            live[count, 5] = meta[origin][meta_row, slots + slot]
            count = count + (slot < meta[origin][meta_row, 2 * slots]).astype(jnp.int32)

    def fetch(i, act):
        for k in range(sources):

            @pl.when(live[i, 0] == k)
            def _():
                act(
                    pltpu.make_async_copy(
                        amps[k].at[pl.ds(pl.multiple_of(live[i, 1], size), size)],
                        amp.at[i % 2],
                        arrived.at[i % 2],
                    )
                )

    @pl.when(count > 0)
    def _():
        fetch(0, lambda copy: copy.start())

    for k in range(held):
        for t in range(cells.shape[2]):
            lanes = slice(t * LANES, (t + 1) * LANES)
            cells[k, :, t, :size, :] = mains[k][:, :, lanes].astype(jnp.float32)
            cells[k, :, t, size:, :] = rims[k][:, :, lanes].astype(jnp.float32)
    if fresh_sums:
        sums[...] = jnp.zeros_like(sums)
    if fresh_grads:
        grads[...] = jnp.zeros_like(grads)
    obj[1] = jnp.zeros_like(obj[1])
    diff[1] = jnp.zeros_like(diff[1])

    lane = lax.broadcasted_iota(jnp.int32, (size, LANES), 1)

    def step(i, carry):
        @pl.when(i < count)
        def _():
            fetch(i, lambda copy: copy.wait())

        @pl.when(i + 1 < count)
        def _():
            fetch(i + 1, lambda copy: copy.start())

        now, before = i % 2, (i + 1) % 2
        this = jnp.minimum(i, jnp.maximum(count - 1, 0))
        last = jnp.maximum(i - 1, 0)
        tile = live[this, 3]
        row = live[this, 4]
        col = live[this, 5]
        back_shift = lax.rem(2 * LANES - col, LANES)
        keep = lane < LANES - col
        for part in range(2):
            rolled = [
                pltpu.roll(cells[tile, part, t, pl.ds(row, size), :], back_shift, 1)
                for t in range(across + 1)
            ]
            for t in range(across):
                obj[now, part, :, t * LANES : (t + 1) * LANES] = jnp.where(
                    keep, rolled[t], rolled[t + 1]
                )
        probe_re, probe_im = probe[0], probe[1]
        obj_re, obj_im = obj[now, 0], obj[now, 1]
        psi = jnp.concatenate(
            [probe_re * obj_re - probe_im * obj_im, probe_re * obj_im + probe_im * obj_re], 0
        ).astype(jnp.bfloat16)
        back = jnp.dot(minus[...], diff[before], preferred_element_type=jnp.float32).astype(
            jnp.bfloat16
        )
        half = jnp.dot(plus[...], psi, preferred_element_type=jnp.float32).astype(jnp.bfloat16)
        change = jnp.dot(
            jnp.concatenate([back[:size], back[size:]], 1),
            plus[...],
            preferred_element_type=jnp.float32,
        )
        spectrum = jnp.dot(
            jnp.concatenate([half[:size], half[size:]], 1),
            minus[...],
            preferred_element_type=jnp.float32,
        )

        old_tile = live[last, 3]
        old_row = live[last, 4]
        old_col = live[last, 5]
        chg_re = change[:, :size]
        chg_im = change[:, size:]
        old_re, old_im = obj[before, 0], obj[before, 1]
        grads[0] += old_re * chg_re + old_im * chg_im
        grads[1] += old_re * chg_im - old_im * chg_re
        ahead = lane >= old_col
        forward_shift = lax.rem(old_col, LANES)
        for part in range(2):
            if part == 0:
                term = probe_re * chg_re + probe_im * chg_im
            else:
                term = probe_re * chg_im - probe_im * chg_re
            rolled = [
                pltpu.roll(term[:, t * LANES : (t + 1) * LANES], forward_shift, 1)
                for t in range(across)
            ]
            for t in range(across + 1):
                if t == 0:
                    piece = jnp.where(ahead, rolled[0], 0.0)
                elif t == across:
                    piece = jnp.where(ahead, 0.0, rolled[t - 1])
                else:
                    piece = jnp.where(ahead, rolled[t], rolled[t - 1])
                sums[old_tile, part, t, pl.ds(old_row, size), :] += piece

        spec_re = spectrum[:, :size]
        spec_im = spectrum[:, size:]
        factor = (
            amp[now].astype(jnp.float32)
            * lax.rsqrt(spec_re * spec_re + spec_im * spec_im + modulus_soft)
            - 1.0
        )
        diff[now, :size, :] = (spec_re * factor).astype(jnp.bfloat16)
        diff[now, size:, :] = (spec_im * factor).astype(jnp.bfloat16)
        return carry

    lax.fori_loop(0, count + 1, step, 0)


def cover(plan, group, metas, amps, tiles, probe, plus, minus, sums=None, grads=None):
    size = probe.shape[1]
    units = len(plan[0](0)) * plan[2]
    mains, rims = [t[0] for t in tiles], [t[1] for t in tiles]
    parts, rows, cols = mains[0].shape
    sums_shape = (len(tiles), parts, cols // LANES, 2 * rows, LANES)
    whole = pl.BlockSpec(memory_space=pltpu.VMEM)
    far = pl.BlockSpec(memory_space=pltpu.HBM)
    operands = [group, *metas, *amps, *mains, *rims, probe, plus, minus]
    aliases = {}
    if sums is not None:
        aliases[len(operands)] = 0
        operands.append(sums)
    if grads is not None:
        aliases[len(operands)] = 1
        operands.append(grads)
    return pl.pallas_call(
        functools.partial(
            position_kernel, plan, len(metas), len(amps), len(tiles), sums is None, grads is None
        ),
        out_shape=(
            jax.ShapeDtypeStruct(sums_shape, jnp.float32),
            jax.ShapeDtypeStruct(probe.shape, jnp.float32),
        ),
        in_specs=[pl.BlockSpec(memory_space=pltpu.SMEM)] * (1 + len(metas))
        + [far] * len(amps)
        + [whole] * (len(operands) - 1 - len(metas) - len(amps)),
        out_specs=(whole, whole),
        input_output_aliases=aliases,
        scratch_shapes=[
            pltpu.VMEM(sums_shape, jnp.float32),
            pltpu.VMEM((2, 2, size, size), jnp.float32),
            pltpu.VMEM((2, 2 * size, size), jnp.bfloat16),
            pltpu.VMEM((2, size, size), jnp.bfloat16),
            pltpu.SMEM((units + 1, 6), jnp.int32),
            pltpu.SemaphoreType.DMA((2,)),
        ],
        compiler_params=pltpu.CompilerParams(vmem_limit_bytes=32 * 1024 * 1024),
        cost_estimate=pl.CostEstimate(
            flops=units // 2 * 4 * 2 * 4 * size * size * size,
            bytes_accessed=units // 2 * 2 * size * size,
            transcendentals=units // 2 * size * size,
        ),
    )(*operands)


def joined(block):
    parts, tiles, rows, lanes = block.shape
    return block.transpose(0, 2, 1, 3).reshape(parts, rows, tiles * lanes)


def swapped(block, blk_bits=0, band_bits=0):
    groups, bands = lax.axis_size("blk"), lax.axis_size("band")
    route = [
        (g * bands + b, (g ^ blk_bits) * bands + (b ^ band_bits))
        for g in range(groups)
        for b in range(bands)
    ]
    return lax.ppermute(block, ("blk", "band"), route)


def turned(block, distance):
    groups = lax.axis_size("blk")
    return lax.ppermute(block, "blk", [(g, (g + 4 * distance) % groups) for g in range(groups)])


def to_next_band(block, blk_bits=0):
    groups, bands = lax.axis_size("blk"), lax.axis_size("band")
    route = [
        (g * bands + b, (g ^ blk_bits) * bands + b + 1)
        for g in range(groups)
        for b in range(bands - 1)
    ]
    return lax.ppermute(block, ("blk", "band"), route)


def summed_everywhere(block):
    parts, rows, cols = block.shape
    group = lax.axis_index("blk")
    line = group // 4
    sides = ((1, group % 2), (4, (line ^ (line // 2)) % 2), (12, line // 2))
    block = block.reshape(parts * rows, cols)
    for bits, side in sides:
        half = block.shape[0] // 2
        kept = lax.dynamic_slice_in_dim(block, side * half, half, 0)
        sent = lax.dynamic_slice_in_dim(block, (1 - side) * half, half, 0)
        block = kept + swapped(sent, bits)
    block = block + swapped(block, 2)
    block = block + swapped(block, 2, 1)
    block = block + swapped(block, 0, 2)
    block = block + swapped(block, 0, 6)
    for bits, side in sides[::-1]:
        other = swapped(block, bits)
        block = jnp.where(
            side == 0,
            jnp.concatenate([block, other], 0),
            jnp.concatenate([other, block], 0),
        )
    return block.reshape(parts, rows, cols)


def own_pairs(group):
    return [(0, 0, group ^ k, group ^ k, k) for k in range(4)]


def line_pairs(group):
    place = group % 4
    return [(k, k, q, q, q ^ place) for k in range(2) for q in range(4)]


def remote_pairs(group):
    return [(0, 0, group ^ 8 ^ k, group ^ 8 ^ k, k) for k in range(2)] + [
        (1, 1, (group ^ k) % 2, (group ^ k) % 2, k) for k in range(2)
    ]


def body(object_band, probe, amplitudes, row_offsets, col_offsets, counts):
    size = probe.shape[1]
    rows_local = object_band.shape[1]
    slots = amplitudes.shape[3]
    bands = lax.axis_size("band")
    groups = lax.axis_size("blk")
    group = lax.axis_index("blk").astype(jnp.int32)
    line = group // 4
    lines = groups // 4
    plus, minus = dft_tables(size)
    own = amplitudes[0, 0]
    by_line = own.reshape(lines, 4, slots, size, size)
    here = group[None]
    many = slots // 2

    rim = lax.ppermute(object_band, "band", [(i, i - 1) for i in range(1, bands)])
    meta = jnp.concatenate([row_offsets[0, 0], col_offsets[0, 0], counts[0, 0][:, None]], 1)

    def message(units, about):
        note = jnp.pad(about, ((0, 16 - about.shape[0]), (0, size - about.shape[1])))
        return jnp.concatenate([units.reshape(-1, size), note.astype(jnp.bfloat16)], 0)

    def noted(received, count):
        return received[-16:, :][:count, : 2 * slots + 1].astype(jnp.int32)

    def chunk(first, last):
        received = []
        for turn in (1, -1):
            to = (line + lines + turn) % lines
            units = lax.dynamic_index_in_dim(by_line, to, 0, False)[:, first:last]
            about = lax.dynamic_slice_in_dim(meta, to * 4, 4, 0)
            received.append(turned(message(units, about), turn))
        return received

    main_side = swapped(object_band, 2)
    main_far = turned(object_band, 2)
    early = chunk(0, many)
    rim_side = swapped(rim, 2)
    rim_far = turned(rim, 2)
    other = (group ^ 10) // 2
    side_amps = swapped(
        message(
            lax.dynamic_index_in_dim(own.reshape(groups // 2, 2, slots, size, size), other, 0, False),
            lax.dynamic_slice_in_dim(meta, other * 2, 2, 0),
        ),
        2,
    )
    near = [
        (object_band, rim),
        (swapped(object_band, 1), swapped(rim, 1)),
        (main_side, rim_side),
        (swapped(main_side, 1), swapped(rim_side, 1)),
    ]
    remote = [(main_far, rim_far), (swapped(main_far, 1), swapped(rim_far, 1))]
    late = chunk(many, slots)
    flat = own.reshape(-1, size)

    meta_lines = [noted(e, 4) for e in early]
    meta_side = noted(side_amps, 2)

    sums, grads = cover((own_pairs, 0, slots), here, [meta], [flat], near, probe, plus, minus)
    remote_sums, grads = cover(
        (remote_pairs, 0, slots),
        here,
        [meta, meta_side],
        [flat, side_amps],
        remote,
        probe,
        plus,
        minus,
        None,
        grads,
    )
    far_total = remote_sums[0] + swapped(remote_sums[1].astype(jnp.bfloat16), 1).astype(
        jnp.float32
    )
    sums, grads = cover(
        (line_pairs, 0, many), here, meta_lines, early, near, probe, plus, minus, sums, grads
    )
    far_total, grads = lax.optimization_barrier((far_total.astype(jnp.bfloat16), grads))
    far_back = turned(far_total, 2)
    sums, grads = cover(
        (line_pairs, many, slots - many),
        here,
        meta_lines,
        late,
        near,
        probe,
        plus,
        minus,
        sums,
        grads,
    )

    crossed = swapped(jnp.stack([sums[1], sums[3]]).astype(jnp.bfloat16), 1).astype(jnp.float32)
    side = (sums[2] + crossed[1]).astype(jnp.bfloat16)
    total = sums[0] + crossed[0] + far_back.astype(jnp.float32)
    side, total, grads = lax.optimization_barrier((side, total, grads))
    side_top = swapped(side[:, :, :rows_local], 2).astype(jnp.float32)
    side_low = to_next_band(side[:, :, rows_local:], 2).astype(jnp.float32)
    low = to_next_band(total[:, :, rows_local:].astype(jnp.bfloat16)).astype(jnp.float32)
    main_sums = joined(total[:, :, :rows_local] + side_top + side_low + low)
    probe_grad = summed_everywhere(grads) / groups
    power = jnp.sum(probe * probe) / (size * size)
    new_object = object_band.astype(jnp.float32) + object_rate * main_sums / (power + 1e-06)
    return (new_object, probe_grad)


def solution(mesh):
    return jax.shard_map(
        body,
        mesh=mesh,
        in_specs=(
            P(None, "band", "blk"),
            P(),
            P("blk", "band", None, None, None, None),
            P("blk", "band", None, None),
            P("blk", "band", None, None),
            P("blk", "band", None),
        ),
        out_specs=(P(None, "band", "blk"), P()),
        check_vma=False,
    )
```

```python
import functools
import math

import jax
import jax.numpy as jnp
from jax import lax
from jax.experimental import pallas as pl
from jax.experimental.pallas import tpu as pltpu
from jax.sharding import PartitionSpec as P

object_rate = 0.5
modulus_soft = 0.5
LANES = 128


def dft_tables(size):
    index_line = jnp.arange(size, dtype=jnp.int32)
    product = index_line[:, None] * index_line[None, :] % size
    angle = product.astype(jnp.float32) * (2.0 * math.pi / size)
    factor = 1.0 / math.sqrt(size)
    cosine = jnp.cos(angle) * factor
    sine = jnp.sin(angle) * factor
    plus = jnp.concatenate(
        [jnp.concatenate([cosine, sine], 1), jnp.concatenate([-sine, cosine], 1)], 0
    ).astype(jnp.bfloat16)
    minus = jnp.concatenate(
        [jnp.concatenate([cosine, -sine], 1), jnp.concatenate([sine, cosine], 1)], 0
    ).astype(jnp.bfloat16)
    return plus, minus


def position_kernel(plan, metas, sources, boards, tiles, fresh_sums, fresh_grads, group_ref, *refs):
    pairs, slots = plan
    meta = refs[:metas]
    amps = refs[metas : metas + sources]
    refs = refs[metas + sources :]
    held = refs[:boards]
    refs = refs[boards:]
    probe, plus, minus = refs[:3]
    refs = refs[3:]
    sums_in = None if fresh_sums else refs[0]
    grads_in = None if fresh_grads else refs[not fresh_sums]
    rest = refs[(not fresh_sums) + (not fresh_grads) :]
    sums, grads, cells, obj, diff, amp, live, arrived = rest
    size = probe.shape[1]
    across = size // LANES
    group = group_ref[0]

    count = jnp.int32(0)
    for origin, source, meta_row, unit_row, tile, first, many in pairs(group, slots):
        for slot in range(first, first + many):
            live[count, 0] = jnp.int32(source)
            live[count, 1] = (unit_row * many + (slot - first)) * size
            live[count, 2] = jnp.int32(0)
            live[count, 3] = tile
            live[count, 4] = meta[origin][meta_row, slot]
            live[count, 5] = meta[origin][meta_row, slots + slot]
            count = count + (slot < meta[origin][meta_row, 2 * slots]).astype(jnp.int32)

    def fetch(i, act):
        for k in range(sources):

            @pl.when(live[i, 0] == k)
            def _():
                act(
                    pltpu.make_async_copy(
                        amps[k].at[pl.ds(pl.multiple_of(live[i, 1], size), size)],
                        amp.at[i % 2],
                        arrived.at[i % 2],
                    )
                )

    @pl.when(count > 0)
    def _():
        fetch(0, lambda copy: copy.start())

    for k, halves in enumerate(tiles):
        for h, (board, spot) in enumerate(halves):
            for t in range(cells.shape[2]):
                lanes = slice(t * LANES, (t + 1) * LANES)
                cells[k, :, t, h * size : (h + 1) * size, :] = held[board][
                    spot, :, :, lanes
                ].astype(jnp.float32)
    sums[...] = jnp.zeros_like(sums) if fresh_sums else sums_in[...]
    grads[...] = jnp.zeros_like(grads) if fresh_grads else grads_in[...]
    obj[1] = jnp.zeros_like(obj[1])
    diff[1] = jnp.zeros_like(diff[1])

    lane = lax.broadcasted_iota(jnp.int32, (size, LANES), 1)

    def step(i, carry):
        @pl.when(i < count)
        def _():
            fetch(i, lambda copy: copy.wait())

        @pl.when(i + 1 < count)
        def _():
            fetch(i + 1, lambda copy: copy.start())

        now, before = i % 2, (i + 1) % 2
        this = jnp.minimum(i, jnp.maximum(count - 1, 0))
        last = jnp.maximum(i - 1, 0)
        tile = live[this, 3]
        row = live[this, 4]
        col = live[this, 5]
        back_shift = lax.rem(2 * LANES - col, LANES)
        keep = lane < LANES - col
        for part in range(2):
            rolled = [
                pltpu.roll(cells[tile, part, t, pl.ds(row, size), :], back_shift, 1)
                for t in range(across + 1)
            ]
            for t in range(across):
                obj[now, part, :, t * LANES : (t + 1) * LANES] = jnp.where(
                    keep, rolled[t], rolled[t + 1]
                )
        probe_re, probe_im = probe[0], probe[1]
        obj_re, obj_im = obj[now, 0], obj[now, 1]
        psi = jnp.concatenate(
            [probe_re * obj_re - probe_im * obj_im, probe_re * obj_im + probe_im * obj_re], 0
        ).astype(jnp.bfloat16)
        back = jnp.dot(minus[...], diff[before], preferred_element_type=jnp.float32).astype(
            jnp.bfloat16
        )
        half = jnp.dot(plus[...], psi, preferred_element_type=jnp.float32).astype(jnp.bfloat16)
        change = jnp.dot(
            jnp.concatenate([back[:size], back[size:]], 1),
            plus[...],
            preferred_element_type=jnp.float32,
        )
        spectrum = jnp.dot(
            jnp.concatenate([half[:size], half[size:]], 1),
            minus[...],
            preferred_element_type=jnp.float32,
        )

        old_tile = live[last, 3]
        old_row = live[last, 4]
        old_col = live[last, 5]
        chg_re = change[:, :size]
        chg_im = change[:, size:]
        old_re, old_im = obj[before, 0], obj[before, 1]
        grads[0] += old_re * chg_re + old_im * chg_im
        grads[1] += old_re * chg_im - old_im * chg_re
        ahead = lane >= old_col
        forward_shift = lax.rem(old_col, LANES)
        for part in range(2):
            if part == 0:
                term = probe_re * chg_re + probe_im * chg_im
            else:
                term = probe_re * chg_im - probe_im * chg_re
            rolled = [
                pltpu.roll(term[:, t * LANES : (t + 1) * LANES], forward_shift, 1)
                for t in range(across)
            ]
            for t in range(across + 1):
                if t == 0:
                    piece = jnp.where(ahead, rolled[0], 0.0)
                elif t == across:
                    piece = jnp.where(ahead, 0.0, rolled[t - 1])
                else:
                    piece = jnp.where(ahead, rolled[t], rolled[t - 1])
                sums[old_tile, part, t, pl.ds(old_row, size), :] += piece

        spec_re = spectrum[:, :size]
        spec_im = spectrum[:, size:]
        factor = (
            amp[now].astype(jnp.float32)
            * lax.rsqrt(spec_re * spec_re + spec_im * spec_im + modulus_soft)
            - 1.0
        )
        diff[now, :size, :] = (spec_re * factor).astype(jnp.bfloat16)
        diff[now, size:, :] = (spec_im * factor).astype(jnp.bfloat16)
        return carry

    lax.fori_loop(0, count + 1, step, 0)


def cover(plan, group, metas, amps, boards, tiles, probe, plus, minus, sums=None, grads=None):
    size = probe.shape[1]
    units = sum(pair[-1] for pair in plan[0](0, plan[1]))
    parts, rows, cols = boards[0].shape[1:]
    cells_shape = (len(tiles), parts, cols // LANES, 2 * rows, LANES)
    sums_shape = cells_shape if sums is None else sums.shape
    whole = pl.BlockSpec(memory_space=pltpu.VMEM)
    far = pl.BlockSpec(memory_space=pltpu.HBM)
    operands = [group, *metas, *amps, *boards, probe, plus, minus]
    aliases = {}
    if sums is not None:
        aliases[len(operands)] = 0
        operands.append(sums)
    if grads is not None:
        aliases[len(operands)] = 1
        operands.append(grads)
    return pl.pallas_call(
        functools.partial(
            position_kernel,
            plan,
            len(metas),
            len(amps),
            len(boards),
            tiles,
            sums is None,
            grads is None,
        ),
        out_shape=(
            jax.ShapeDtypeStruct(sums_shape, jnp.float32),
            jax.ShapeDtypeStruct(probe.shape, jnp.float32),
        ),
        in_specs=[pl.BlockSpec(memory_space=pltpu.SMEM)] * (1 + len(metas))
        + [far] * len(amps)
        + [whole] * (len(operands) - 1 - len(metas) - len(amps)),
        out_specs=(whole, whole),
        input_output_aliases=aliases,
        scratch_shapes=[
            pltpu.VMEM(cells_shape, jnp.float32),
            pltpu.VMEM((2, 2, size, size), jnp.float32),
            pltpu.VMEM((2, 2 * size, size), jnp.bfloat16),
            pltpu.VMEM((2, size, size), jnp.bfloat16),
            pltpu.SMEM((units + 1, 6), jnp.int32),
            pltpu.SemaphoreType.DMA((2,)),
        ],
        compiler_params=pltpu.CompilerParams(vmem_limit_bytes=32 * 1024 * 1024),
        cost_estimate=pl.CostEstimate(
            flops=units // 2 * 4 * 2 * 4 * size * size * size,
            bytes_accessed=units // 2 * 2 * size * size,
            transcendentals=units // 2 * size * size,
        ),
    )(*operands)


def joined(block):
    parts, tiles, rows, lanes = block.shape
    return block.transpose(0, 2, 1, 3).reshape(parts, rows, tiles * lanes)


def swapped(block, blk_bits=0, band_bits=0):
    groups, bands = lax.axis_size("blk"), lax.axis_size("band")
    route = [
        (g * bands + b, (g ^ blk_bits) * bands + (b ^ band_bits))
        for g in range(groups)
        for b in range(bands)
    ]
    return lax.ppermute(block, ("blk", "band"), route)


def turned(block, distance):
    groups = lax.axis_size("blk")
    return lax.ppermute(block, "blk", [(g, (g + 4 * distance) % groups) for g in range(groups)])


def to_next_band(block, blk_bits=0):
    groups, bands = lax.axis_size("blk"), lax.axis_size("band")
    route = [
        (g * bands + b, (g ^ blk_bits) * bands + b + 1)
        for g in range(groups)
        for b in range(bands - 1)
    ]
    return lax.ppermute(block, ("blk", "band"), route)


def to_previous_band(block, blk_bits=0):
    groups, bands = lax.axis_size("blk"), lax.axis_size("band")
    route = [
        (g * bands + b, (g ^ blk_bits) * bands + b - 1)
        for g in range(groups)
        for b in range(1, bands)
    ]
    return lax.ppermute(block, ("blk", "band"), route)


def summed_everywhere(block, beside):
    parts, rows, cols = block.shape
    depth = lax.axis_index("band") // 2
    sides = (
        (1, 0, lax.axis_index("blk") % 2),
        (0, 2, (depth ^ (depth // 2)) % 2),
        (0, 6, depth // 2),
    )
    block = block.reshape(parts * rows, cols)
    for blk_bits, band_bits, side in sides:
        half = block.shape[0] // 2
        kept = lax.dynamic_slice_in_dim(block, side * half, half, 0)
        sent = lax.dynamic_slice_in_dim(block, (1 - side) * half, half, 0)
        block = kept + swapped(sent, blk_bits, band_bits)
    for blk_bits, band_bits in ((4, 0), (12, 0)):
        block = block + swapped(block, blk_bits, band_bits)
    block, beside = lax.optimization_barrier((block, beside))
    for blk_bits, band_bits in ((2, 0), (2, 1)):
        block = block + swapped(block, blk_bits, band_bits)
    for blk_bits, band_bits, side in sides[::-1]:
        other = swapped(block, blk_bits, band_bits)
        block = jnp.where(
            side == 0,
            jnp.concatenate([block, other], 0),
            jnp.concatenate([other, block], 0),
        )
    return block.reshape(parts, rows, cols), beside


def first_pairs(group, slots):
    return [
        (0, 0, group, group, 0, 0, slots),
        (0, 0, group ^ 2, group ^ 2, 1, 0, slots),
        (1, 1, group, group // 2, 0, 0, slots),
        (1, 1, group ^ 2, (group ^ 2) // 2, 1, 0, slots),
        (2, 2, 0, 0, 1, 0, slots),
        (3, 3, 0, 0, 1, 0, slots),
    ]


def second_pairs(group, slots):
    return [(k, k, 0, 0, 1, 0, slots) for k in range(2)]


def far_pairs(group, slots):
    return [
        (0, 0, group ^ 8, group ^ 8, 0, 0, slots),
        (1, 1, group ^ 8, (group ^ 8) // 2, 0, 0, slots),
    ] + [(2, 2, source, source, 0, 0, slots) for source in range(2)]


def last_pairs(group, slots):
    return [(k, k, source, source, 0, 0, slots) for k in range(2) for source in range(2)]


def body(object_band, probe, amplitudes, row_offsets, col_offsets, counts):
    size = probe.shape[1]
    rows_local = object_band.shape[1]
    slots = amplitudes.shape[3]
    bands = lax.axis_size("band")
    groups = lax.axis_size("blk")
    group = lax.axis_index("blk").astype(jnp.int32)
    line = group // 4
    lines = groups // 4
    plus, minus = dft_tables(size)
    own = amplitudes[0, 0]
    here = group[None]

    core = group % 2
    core, across = group % 2, group // 2 % 2
    paired = own.reshape(groups // 2, 2, slots, size, size)
    meta = jnp.concatenate([row_offsets[0, 0], col_offsets[0, 0], counts[0, 0][:, None]], 1)

    def units(spot, parity, source=paired):
        return lax.dynamic_slice(source, (spot, parity, 0, 0, 0), (1, 1, slots, size, size))[0]

    def notes(about, spot):
        return lax.dynamic_slice_in_dim(about, spot * 2 + core, 1, 0)

    def message(pieces, abouts):
        about = jnp.concatenate(abouts, 0)
        note = jnp.pad(about, ((0, 16 - about.shape[0]), (0, size - about.shape[1])))
        rows = [p.reshape(-1, size) for p in pieces]
        return jnp.concatenate([*rows, note.astype(jnp.bfloat16)], 0)

    def noted(received, count):
        return received[-16:, :][:count, : 2 * slots + 1].astype(jnp.int32)

    turns = (1, -1)
    ends = [(line + lines + turn) % lines * 2 for turn in turns]
    opposite = (line + 2) % lines * 2
    pieces = [message([units(e + 1 - across, core)], [notes(meta, e + 1 - across)]) for e in ends]
    rim = to_previous_band(object_band)
    early = [turned(piece, turn) for piece, turn in zip(pieces, turns)]
    main_side = swapped(object_band, 2)
    rim_side = to_previous_band(object_band, 2)
    meta_next = swapped(meta, 1)
    pieces, paired_then = lax.optimization_barrier((pieces, paired))
    theirs = swapped(lax.dynamic_index_in_dim(paired_then, 1 - core, 1, False), 1)

    def next_units(spot, source=theirs):
        return lax.dynamic_index_in_dim(source, spot, 0)

    early += [
        turned(
            message([next_units(e + 1 - across)], [notes(meta_next, e + 1 - across)]), turn
        )
        for e, turn in zip(ends, turns)
    ]
    beyond = opposite + 1 - across
    side_amps = swapped(
        message(
            [units(beyond, core), next_units(beyond)],
            [notes(meta, beyond), notes(meta_next, beyond)],
        ),
        2,
    )

    rim_then, early = lax.optimization_barrier((rim, early))
    far_board = turned(jnp.stack([object_band, rim_then]), 2)
    near = [object_band[None], rim[None], main_side[None], rim_side[None]]
    near_tiles = (((0, 0), (1, 0)), ((2, 0), (3, 0)))
    far_tiles = (((0, 0), (0, 1)),)
    flat = own.reshape(-1, size)
    theirs_flat = theirs.reshape(-1, size)

    meta_lines = [noted(e, 1) for e in early]
    meta_side = noted(side_amps, 2)
    tables = (probe, plus, minus)

    sums, grads = cover(
        (first_pairs, slots),
        here,
        [meta, meta_next, *meta_lines[:2]],
        [flat, theirs_flat, *early[:2]],
        near,
        near_tiles,
        *tables,
    )
    early, paired_late, theirs_late = lax.optimization_barrier((early, paired, theirs))
    late = [
        turned(
            message(
                [units(spot, core, paired_late), next_units(spot, theirs_late)],
                [notes(meta, spot), notes(meta_next, spot)],
            ),
            turn,
        )
        for spot, turn in zip([e + across for e in ends], turns)
    ]
    sums, grads = cover(
        (second_pairs, slots),
        here,
        meta_lines[2:],
        early[2:],
        near,
        near_tiles,
        *tables,
        sums,
        grads,
    )
    side = sums[1].astype(jnp.bfloat16)
    side, late, grads = lax.optimization_barrier((side, late, grads))
    side = swapped(side, 2)
    far_sums, grads = cover(
        (far_pairs, slots),
        here,
        [meta, meta_next, meta_side],
        [flat, theirs_flat, side_amps],
        [far_board],
        far_tiles,
        *tables,
        None,
        grads,
    )
    far_back = far_sums[0].astype(jnp.bfloat16)
    far_back, side, grads = lax.optimization_barrier((far_back, side, grads))
    far_back = turned(far_back, 2)
    sums, grads = cover(
        (last_pairs, slots),
        here,
        [noted(e, 2) for e in late],
        late,
        near[:2],
        near_tiles[:1],
        *tables,
        sums,
        grads,
    )

    far_back, grads = lax.optimization_barrier((far_back, grads))
    total = sums[0] + far_back.astype(jnp.float32) + side.astype(jnp.float32)
    low = to_next_band(total[:, :, rows_local:].astype(jnp.bfloat16))
    probe_sum, low = summed_everywhere(grads, low)
    main_sums = joined(total[:, :, :rows_local] + low.astype(jnp.float32))
    probe_grad = probe_sum / groups
    power = jnp.sum(probe * probe) / (size * size)
    new_object = object_band.astype(jnp.float32) + object_rate * main_sums / (power + 1e-06)
    return (new_object, probe_grad)


def solution(mesh):
    return jax.shard_map(
        body,
        mesh=mesh,
        in_specs=(
            P(None, "band", "blk"),
            P(),
            P("blk", "band", None, None, None, None),
            P("blk", "band", None, None),
            P("blk", "band", None, None),
            P("blk", "band", None),
        ),
        out_specs=(P(None, "band", "blk"), P()),
        check_vma=False,
    )
```

```python
import functools
import math

import jax
import jax.numpy as jnp
from jax import lax
from jax.experimental import pallas as pl
from jax.experimental.pallas import tpu as pltpu
from jax.sharding import PartitionSpec as P

object_rate = 0.5
modulus_soft = 0.5
LANES = 128


def dft_tables(size):
    index_line = jnp.arange(size, dtype=jnp.int32)
    product = index_line[:, None] * index_line[None, :] % size
    angle = product.astype(jnp.float32) * (2.0 * math.pi / size)
    factor = 1.0 / math.sqrt(size)
    cosine = jnp.cos(angle) * factor
    sine = jnp.sin(angle) * factor
    plus = jnp.concatenate(
        [jnp.concatenate([cosine, sine], 1), jnp.concatenate([-sine, cosine], 1)], 0
    ).astype(jnp.bfloat16)
    minus = jnp.concatenate(
        [jnp.concatenate([cosine, -sine], 1), jnp.concatenate([sine, cosine], 1)], 0
    ).astype(jnp.bfloat16)
    return plus, minus


def position_kernel(plan, metas, sources, boards, tiles, fresh_sums, fresh_grads, group_ref, *refs):
    pairs, slots = plan
    meta = refs[:metas]
    amps = refs[metas : metas + sources]
    refs = refs[metas + sources :]
    held = refs[:boards]
    refs = refs[boards:]
    probe, plus, minus = refs[:3]
    refs = refs[3:]
    sums_in = None if fresh_sums else refs[0]
    grads_in = None if fresh_grads else refs[not fresh_sums]
    rest = refs[(not fresh_sums) + (not fresh_grads) :]
    sums, grads, cells, obj, diff, amp, live, arrived = rest
    size = probe.shape[1]
    across = size // LANES
    group = group_ref[0]

    count = jnp.int32(0)
    for origin, source, meta_row, unit_row, tile, first, many in pairs(group, slots):
        for slot in range(first, first + many):
            live[count, 0] = jnp.int32(source)
            live[count, 1] = (unit_row * many + (slot - first)) * size
            live[count, 2] = jnp.int32(0)
            live[count, 3] = tile
            live[count, 4] = meta[origin][meta_row, slot]
            live[count, 5] = meta[origin][meta_row, slots + slot]
            count = count + (slot < meta[origin][meta_row, 2 * slots]).astype(jnp.int32)

    def fetch(i, act):
        for k in range(sources):

            @pl.when(live[i, 0] == k)
            def _():
                act(
                    pltpu.make_async_copy(
                        amps[k].at[pl.ds(pl.multiple_of(live[i, 1], size), size)],
                        amp.at[i % 2],
                        arrived.at[i % 2],
                    )
                )

    @pl.when(count > 0)
    def _():
        fetch(0, lambda copy: copy.start())

    for k, halves in enumerate(tiles):
        for h, (board, spot) in enumerate(halves):
            for t in range(cells.shape[2]):
                lanes = slice(t * LANES, (t + 1) * LANES)
                cells[k, :, t, h * size : (h + 1) * size, :] = held[board][
                    spot, :, :, lanes
                ].astype(jnp.float32)
    sums[...] = jnp.zeros_like(sums) if fresh_sums else sums_in[...]
    grads[...] = jnp.zeros_like(grads) if fresh_grads else grads_in[...]
    obj[1] = jnp.zeros_like(obj[1])
    diff[1] = jnp.zeros_like(diff[1])

    lane = lax.broadcasted_iota(jnp.int32, (size, LANES), 1)

    def step(i, carry):
        @pl.when(i < count)
        def _():
            fetch(i, lambda copy: copy.wait())

        @pl.when(i + 1 < count)
        def _():
            fetch(i + 1, lambda copy: copy.start())

        now, before = i % 2, (i + 1) % 2
        this = jnp.minimum(i, jnp.maximum(count - 1, 0))
        last = jnp.maximum(i - 1, 0)
        tile = live[this, 3]
        row = live[this, 4]
        col = live[this, 5]
        back_shift = lax.rem(2 * LANES - col, LANES)
        keep = lane < LANES - col
        for part in range(2):
            rolled = [
                pltpu.roll(cells[tile, part, t, pl.ds(row, size), :], back_shift, 1)
                for t in range(across + 1)
            ]
            for t in range(across):
                obj[now, part, :, t * LANES : (t + 1) * LANES] = jnp.where(
                    keep, rolled[t], rolled[t + 1]
                )
        probe_re, probe_im = probe[0], probe[1]
        obj_re, obj_im = obj[now, 0], obj[now, 1]
        psi = jnp.concatenate(
            [probe_re * obj_re - probe_im * obj_im, probe_re * obj_im + probe_im * obj_re], 0
        ).astype(jnp.bfloat16)
        back = jnp.dot(minus[...], diff[before], preferred_element_type=jnp.float32).astype(
            jnp.bfloat16
        )
        half = jnp.dot(plus[...], psi, preferred_element_type=jnp.float32).astype(jnp.bfloat16)
        change = jnp.dot(
            jnp.concatenate([back[:size], back[size:]], 1),
            plus[...],
            preferred_element_type=jnp.float32,
        )
        spectrum = jnp.dot(
            jnp.concatenate([half[:size], half[size:]], 1),
            minus[...],
            preferred_element_type=jnp.float32,
        )

        old_tile = live[last, 3]
        old_row = live[last, 4]
        old_col = live[last, 5]
        chg_re = change[:, :size]
        chg_im = change[:, size:]
        old_re, old_im = obj[before, 0], obj[before, 1]
        grads[0] += old_re * chg_re + old_im * chg_im
        grads[1] += old_re * chg_im - old_im * chg_re
        ahead = lane >= old_col
        forward_shift = lax.rem(old_col, LANES)
        for part in range(2):
            if part == 0:
                term = probe_re * chg_re + probe_im * chg_im
            else:
                term = probe_re * chg_im - probe_im * chg_re
            rolled = [
                pltpu.roll(term[:, t * LANES : (t + 1) * LANES], forward_shift, 1)
                for t in range(across)
            ]
            for t in range(across + 1):
                if t == 0:
                    piece = jnp.where(ahead, rolled[0], 0.0)
                elif t == across:
                    piece = jnp.where(ahead, 0.0, rolled[t - 1])
                else:
                    piece = jnp.where(ahead, rolled[t], rolled[t - 1])
                sums[old_tile, part, t, pl.ds(old_row, size), :] += piece

        spec_re = spectrum[:, :size]
        spec_im = spectrum[:, size:]
        factor = (
            amp[now].astype(jnp.float32)
            * lax.rsqrt(spec_re * spec_re + spec_im * spec_im + modulus_soft)
            - 1.0
        )
        diff[now, :size, :] = (spec_re * factor).astype(jnp.bfloat16)
        diff[now, size:, :] = (spec_im * factor).astype(jnp.bfloat16)
        return carry

    lax.fori_loop(0, count + 1, step, 0)


def cover(plan, group, metas, amps, boards, tiles, probe, plus, minus, sums=None, grads=None):
    size = probe.shape[1]
    units = sum(pair[-1] for pair in plan[0](0, plan[1]))
    parts, rows, cols = boards[0].shape[1:]
    cells_shape = (len(tiles), parts, cols // LANES, 2 * rows, LANES)
    sums_shape = cells_shape if sums is None else sums.shape
    whole = pl.BlockSpec(memory_space=pltpu.VMEM)
    far = pl.BlockSpec(memory_space=pltpu.HBM)
    operands = [group, *metas, *amps, *boards, probe, plus, minus]
    aliases = {}
    if sums is not None:
        aliases[len(operands)] = 0
        operands.append(sums)
    if grads is not None:
        aliases[len(operands)] = 1
        operands.append(grads)
    return pl.pallas_call(
        functools.partial(
            position_kernel,
            plan,
            len(metas),
            len(amps),
            len(boards),
            tiles,
            sums is None,
            grads is None,
        ),
        out_shape=(
            jax.ShapeDtypeStruct(sums_shape, jnp.float32),
            jax.ShapeDtypeStruct(probe.shape, jnp.float32),
        ),
        in_specs=[pl.BlockSpec(memory_space=pltpu.SMEM)] * (1 + len(metas))
        + [far] * len(amps)
        + [whole] * (len(operands) - 1 - len(metas) - len(amps)),
        out_specs=(whole, whole),
        input_output_aliases=aliases,
        scratch_shapes=[
            pltpu.VMEM(cells_shape, jnp.float32),
            pltpu.VMEM((2, 2, size, size), jnp.float32),
            pltpu.VMEM((2, 2 * size, size), jnp.bfloat16),
            pltpu.VMEM((2, size, size), jnp.bfloat16),
            pltpu.SMEM((units + 1, 6), jnp.int32),
            pltpu.SemaphoreType.DMA((2,)),
        ],
        compiler_params=pltpu.CompilerParams(vmem_limit_bytes=32 * 1024 * 1024),
        cost_estimate=pl.CostEstimate(
            flops=units // 2 * 4 * 2 * 4 * size * size * size,
            bytes_accessed=units // 2 * 2 * size * size,
            transcendentals=units // 2 * size * size,
        ),
    )(*operands)


def joined(block):
    parts, tiles, rows, lanes = block.shape
    return block.transpose(0, 2, 1, 3).reshape(parts, rows, tiles * lanes)


def swapped(block, blk_bits=0, band_bits=0):
    groups, bands = lax.axis_size("blk"), lax.axis_size("band")
    route = [
        (g * bands + b, (g ^ blk_bits) * bands + (b ^ band_bits))
        for g in range(groups)
        for b in range(bands)
    ]
    return lax.ppermute(block, ("blk", "band"), route)


def turned(block, distance):
    groups = lax.axis_size("blk")
    return lax.ppermute(block, "blk", [(g, (g + 4 * distance) % groups) for g in range(groups)])


def to_next_band(block, blk_bits=0):
    groups, bands = lax.axis_size("blk"), lax.axis_size("band")
    route = [
        (g * bands + b, (g ^ blk_bits) * bands + b + 1)
        for g in range(groups)
        for b in range(bands - 1)
    ]
    return lax.ppermute(block, ("blk", "band"), route)


def to_previous_band(block, blk_bits=0):
    groups, bands = lax.axis_size("blk"), lax.axis_size("band")
    route = [
        (g * bands + b, (g ^ blk_bits) * bands + b - 1)
        for g in range(groups)
        for b in range(1, bands)
    ]
    return lax.ppermute(block, ("blk", "band"), route)


def summed_everywhere(block, beside):
    parts, rows, cols = block.shape
    depth = lax.axis_index("band") // 2
    sides = (
        (1, 0, lax.axis_index("blk") % 2),
        (0, 2, (depth ^ (depth // 2)) % 2),
        (0, 6, depth // 2),
    )
    block = block.reshape(parts * rows, cols)
    for blk_bits, band_bits, side in sides:
        half = block.shape[0] // 2
        kept = lax.dynamic_slice_in_dim(block, side * half, half, 0)
        sent = lax.dynamic_slice_in_dim(block, (1 - side) * half, half, 0)
        block = kept + swapped(sent, blk_bits, band_bits)
    for blk_bits, band_bits in ((4, 0), (12, 0)):
        block = block + swapped(block, blk_bits, band_bits)
    block, beside = lax.optimization_barrier((block, beside))
    for blk_bits, band_bits in ((2, 0), (2, 1)):
        block = block + swapped(block, blk_bits, band_bits)
    for blk_bits, band_bits, side in sides[::-1]:
        other = swapped(block, blk_bits, band_bits)
        block = jnp.where(
            side == 0,
            jnp.concatenate([block, other], 0),
            jnp.concatenate([other, block], 0),
        )
    return block.reshape(parts, rows, cols), beside


def near_pairs(group, slots):
    return [
        (0, 0, group, group, 0, 0, slots),
        (0, 0, group ^ 2, group ^ 2, 1, 0, slots),
        (1, 1, group, group // 2, 0, 0, slots),
        (1, 1, group ^ 2, (group ^ 2) // 2, 1, 0, slots),
    ] + [(2 + k, 2 + k, 0, 0, 1, 0, slots) for k in range(4)]


def far_pairs(group, slots):
    return [
        (0, 0, group ^ 8, group ^ 8, 0, 0, slots),
        (1, 1, group ^ 8, (group ^ 8) // 2, 0, 0, slots),
    ] + [(2, 2, source, source, 0, 0, slots) for source in range(2)]


def last_pairs(group, slots):
    return [(k, k, 0, 0, 0, 0, slots) for k in range(4)]


def body(object_band, probe, amplitudes, row_offsets, col_offsets, counts):
    size = probe.shape[1]
    rows_local = object_band.shape[1]
    slots = amplitudes.shape[3]
    bands = lax.axis_size("band")
    groups = lax.axis_size("blk")
    group = lax.axis_index("blk").astype(jnp.int32)
    line = group // 4
    lines = groups // 4
    plus, minus = dft_tables(size)
    own = amplitudes[0, 0]
    here = group[None]

    core = group % 2
    core, across = group % 2, group // 2 % 2
    paired = own.reshape(groups // 2, 2, slots, size, size)
    meta = jnp.concatenate([row_offsets[0, 0], col_offsets[0, 0], counts[0, 0][:, None]], 1)

    def units(spot, parity, source=paired):
        return lax.dynamic_slice(source, (spot, parity, 0, 0, 0), (1, 1, slots, size, size))[0]

    def notes(about, spot):
        return lax.dynamic_slice_in_dim(about, spot * 2 + core, 1, 0)

    def message(pieces, abouts):
        about = jnp.concatenate(abouts, 0)
        note = jnp.pad(about, ((0, 16 - about.shape[0]), (0, size - about.shape[1])))
        rows = [p.reshape(-1, size) for p in pieces]
        return jnp.concatenate([*rows, note.astype(jnp.bfloat16)], 0)

    def noted(received, count):
        return received[-16:, :][:count, : 2 * slots + 1].astype(jnp.int32)

    turns = (1, -1)
    ends = [(line + lines + turn) % lines * 2 for turn in turns]
    opposite = (line + 2) % lines * 2
    pieces = [message([units(e + 1 - across, core)], [notes(meta, e + 1 - across)]) for e in ends]
    rim = to_previous_band(object_band)
    early = [turned(piece, turn) for piece, turn in zip(pieces, turns)]
    main_side = swapped(object_band, 2)
    rim_side = to_previous_band(object_band, 2)
    meta_next = swapped(meta, 1)
    pieces, paired_then = lax.optimization_barrier((pieces, paired))
    theirs = swapped(lax.dynamic_index_in_dim(paired_then, 1 - core, 1, False), 1)

    def next_units(spot, source=theirs):
        return lax.dynamic_index_in_dim(source, spot, 0)

    early += [
        turned(
            message([next_units(e + 1 - across)], [notes(meta_next, e + 1 - across)]), turn
        )
        for e, turn in zip(ends, turns)
    ]
    beyond = opposite + 1 - across
    side_amps = swapped(
        message(
            [units(beyond, core), next_units(beyond)],
            [notes(meta, beyond), notes(meta_next, beyond)],
        ),
        2,
    )

    rim_then, early = lax.optimization_barrier((rim, early))
    far_board = turned(jnp.stack([object_band, rim_then]), 2)
    tile = (((0, 0), (1, 0)),)
    far_tile = (((0, 0), (0, 1)),)
    flat = own.reshape(-1, size)
    theirs_flat = theirs.reshape(-1, size)

    meta_lines = [noted(e, 1) for e in early]
    meta_side = noted(side_amps, 2)
    tables = (probe, plus, minus)

    early, paired_late, theirs_late = lax.optimization_barrier((early, paired, theirs))
    spots = [e + across for e in ends]
    late = [
        turned(message([units(spot, core, paired_late)], [notes(meta, spot)]), turn)
        for spot, turn in zip(spots, turns)
    ]
    sums, grads = cover(
        (near_pairs, slots),
        here,
        [meta, meta_next, *meta_lines],
        [flat, theirs_flat, *early],
        [object_band[None], rim[None], main_side[None], rim_side[None]],
        (((0, 0), (1, 0)), ((2, 0), (3, 0))),
        *tables,
    )
    side = sums[1].astype(jnp.bfloat16)
    side, late, theirs_late, grads = lax.optimization_barrier((side, late, theirs_late, grads))
    side = swapped(side, 2)
    late += [
        turned(message([next_units(spot, theirs_late)], [notes(meta_next, spot)]), turn)
        for spot, turn in zip(spots, turns)
    ]
    far_sums, grads = cover(
        (far_pairs, slots),
        here,
        [meta, meta_next, meta_side],
        [flat, theirs_flat, side_amps],
        [far_board],
        far_tile,
        *tables,
        None,
        grads,
    )
    far_back = far_sums[0].astype(jnp.bfloat16)
    far_back, side, grads = lax.optimization_barrier((far_back, side, grads))
    far_back = turned(far_back, 2)
    sums, grads = cover(
        (last_pairs, slots),
        here,
        [noted(e, 1) for e in late],
        late,
        [object_band[None], rim[None]],
        tile,
        *tables,
        sums,
        grads,
    )

    far_back, grads = lax.optimization_barrier((far_back, grads))
    total = sums[0] + far_back.astype(jnp.float32) + side.astype(jnp.float32)
    low = to_next_band(total[:, :, rows_local:].astype(jnp.bfloat16))
    probe_sum, low = summed_everywhere(grads, low)
    main_sums = joined(total[:, :, :rows_local] + low.astype(jnp.float32))
    probe_grad = probe_sum / groups
    power = jnp.sum(probe * probe) / (size * size)
    new_object = object_band.astype(jnp.float32) + object_rate * main_sums / (power + 1e-06)
    return (new_object, probe_grad)


def solution(mesh):
    return jax.shard_map(
        body,
        mesh=mesh,
        in_specs=(
            P(None, "band", "blk"),
            P(),
            P("blk", "band", None, None, None, None),
            P("blk", "band", None, None),
            P("blk", "band", None, None),
            P("blk", "band", None),
        ),
        out_specs=(P(None, "band", "blk"), P()),
        check_vma=False,
    )
```

```python
import functools
import math

import jax
import jax.numpy as jnp
from jax import lax
from jax.experimental import pallas as pl
from jax.experimental.pallas import tpu as pltpu
from jax.sharding import PartitionSpec as P

object_rate = 0.5
modulus_soft = 0.5
LANES = 128


def dft_tables(size):
    index_line = jnp.arange(size, dtype=jnp.int32)
    product = index_line[:, None] * index_line[None, :] % size
    angle = product.astype(jnp.float32) * (2.0 * math.pi / size)
    factor = 1.0 / math.sqrt(size)
    cosine = jnp.cos(angle) * factor
    sine = jnp.sin(angle) * factor
    plus = jnp.concatenate(
        [jnp.concatenate([cosine, sine], 1), jnp.concatenate([-sine, cosine], 1)], 0
    ).astype(jnp.bfloat16)
    minus = jnp.concatenate(
        [jnp.concatenate([cosine, -sine], 1), jnp.concatenate([sine, cosine], 1)], 0
    ).astype(jnp.bfloat16)
    return plus, minus


def position_kernel(plan, metas, sources, boards, tiles, fresh_sums, fresh_grads, group_ref, *refs):
    pairs, slots = plan
    meta = refs[:metas]
    amps = refs[metas : metas + sources]
    refs = refs[metas + sources :]
    held = refs[:boards]
    refs = refs[boards:]
    probe, plus, minus = refs[:3]
    refs = refs[3:]
    sums_in = None if fresh_sums else refs[0]
    grads_in = None if fresh_grads else refs[not fresh_sums]
    rest = refs[(not fresh_sums) + (not fresh_grads) :]
    sums, grads, cells, obj, diff, amp, live, arrived = rest
    size = probe.shape[1]
    across = size // LANES
    group = group_ref[0]

    count = jnp.int32(0)
    for origin, source, meta_row, unit_row, tile, first, many in pairs(group, slots):
        for slot in range(first, first + many):
            live[count, 0] = jnp.int32(source)
            live[count, 1] = (unit_row * many + (slot - first)) * size
            live[count, 2] = jnp.int32(0)
            live[count, 3] = tile
            live[count, 4] = meta[origin][meta_row, slot]
            live[count, 5] = meta[origin][meta_row, slots + slot]
            count = count + (slot < meta[origin][meta_row, 2 * slots]).astype(jnp.int32)

    def fetch(i, act):
        for k in range(sources):

            @pl.when(live[i, 0] == k)
            def _():
                act(
                    pltpu.make_async_copy(
                        amps[k].at[pl.ds(pl.multiple_of(live[i, 1], size), size)],
                        amp.at[i % 2],
                        arrived.at[i % 2],
                    )
                )

    @pl.when(count > 0)
    def _():
        fetch(0, lambda copy: copy.start())

    for k, halves in enumerate(tiles):
        for h, (board, spot) in enumerate(halves):
            for t in range(cells.shape[2]):
                lanes = slice(t * LANES, (t + 1) * LANES)
                cells[k, :, t, h * size : (h + 1) * size, :] = held[board][
                    spot, :, :, lanes
                ].astype(jnp.float32)
    sums[...] = jnp.zeros_like(sums) if fresh_sums else sums_in[...]
    grads[...] = jnp.zeros_like(grads) if fresh_grads else grads_in[...]
    obj[1] = jnp.zeros_like(obj[1])
    diff[1] = jnp.zeros_like(diff[1])

    lane = lax.broadcasted_iota(jnp.int32, (size, LANES), 1)

    def step(i, carry):
        @pl.when(i < count)
        def _():
            fetch(i, lambda copy: copy.wait())

        @pl.when(i + 1 < count)
        def _():
            fetch(i + 1, lambda copy: copy.start())

        now, before = i % 2, (i + 1) % 2
        this = jnp.minimum(i, jnp.maximum(count - 1, 0))
        last = jnp.maximum(i - 1, 0)
        back = jnp.dot(minus[...], diff[before], preferred_element_type=jnp.float32).astype(
            jnp.bfloat16
        )
        tile = live[this, 3]
        row = live[this, 4]
        col = live[this, 5]
        back_shift = lax.rem(2 * LANES - col, LANES)
        keep = lane < LANES - col
        for part in range(2):
            rolled = [
                pltpu.roll(cells[tile, part, t, pl.ds(row, size), :], back_shift, 1)
                for t in range(across + 1)
            ]
            for t in range(across):
                obj[now, part, :, t * LANES : (t + 1) * LANES] = jnp.where(
                    keep, rolled[t], rolled[t + 1]
                )
        probe_re, probe_im = probe[0], probe[1]
        obj_re, obj_im = obj[now, 0], obj[now, 1]
        psi = jnp.concatenate(
            [probe_re * obj_re - probe_im * obj_im, probe_re * obj_im + probe_im * obj_re], 0
        ).astype(jnp.bfloat16)
        change = jnp.dot(
            jnp.concatenate([back[:size], back[size:]], 1),
            plus[...],
            preferred_element_type=jnp.float32,
        )
        half = jnp.dot(plus[...], psi, preferred_element_type=jnp.float32).astype(jnp.bfloat16)
        old_tile = live[last, 3]
        old_row = live[last, 4]
        old_col = live[last, 5]
        chg_re = change[:, :size]
        chg_im = change[:, size:]
        old_re, old_im = obj[before, 0], obj[before, 1]
        grads[0] += old_re * chg_re + old_im * chg_im
        grads[1] += old_re * chg_im - old_im * chg_re
        ahead = lane >= old_col
        forward_shift = lax.rem(old_col, LANES)
        for part in range(2):
            if part == 0:
                term = probe_re * chg_re + probe_im * chg_im
            else:
                term = probe_re * chg_im - probe_im * chg_re
            rolled = [
                pltpu.roll(term[:, t * LANES : (t + 1) * LANES], forward_shift, 1)
                for t in range(across)
            ]
            for t in range(across + 1):
                if t == 0:
                    piece = jnp.where(ahead, rolled[0], 0.0)
                elif t == across:
                    piece = jnp.where(ahead, 0.0, rolled[t - 1])
                else:
                    piece = jnp.where(ahead, rolled[t], rolled[t - 1])
                sums[old_tile, part, t, pl.ds(old_row, size), :] += piece

        spectrum = jnp.dot(
            jnp.concatenate([half[:size], half[size:]], 1),
            minus[...],
            preferred_element_type=jnp.float32,
        )

        spec_re = spectrum[:, :size]
        spec_im = spectrum[:, size:]
        factor = (
            amp[now].astype(jnp.float32)
            * lax.rsqrt(spec_re * spec_re + spec_im * spec_im + modulus_soft)
            - 1.0
        )
        diff[now, :size, :] = (spec_re * factor).astype(jnp.bfloat16)
        diff[now, size:, :] = (spec_im * factor).astype(jnp.bfloat16)
        return carry

    lax.fori_loop(0, count + 1, step, 0)


def cover(plan, group, metas, amps, boards, tiles, probe, plus, minus, sums=None, grads=None):
    size = probe.shape[1]
    units = sum(pair[-1] for pair in plan[0](0, plan[1]))
    parts, rows, cols = boards[0].shape[1:]
    cells_shape = (len(tiles), parts, cols // LANES, 2 * rows, LANES)
    sums_shape = cells_shape if sums is None else sums.shape
    whole = pl.BlockSpec(memory_space=pltpu.VMEM)
    far = pl.BlockSpec(memory_space=pltpu.HBM)
    operands = [group, *metas, *amps, *boards, probe, plus, minus]
    aliases = {}
    if sums is not None:
        aliases[len(operands)] = 0
        operands.append(sums)
    if grads is not None:
        aliases[len(operands)] = 1
        operands.append(grads)
    return pl.pallas_call(
        functools.partial(
            position_kernel,
            plan,
            len(metas),
            len(amps),
            len(boards),
            tiles,
            sums is None,
            grads is None,
        ),
        out_shape=(
            jax.ShapeDtypeStruct(sums_shape, jnp.float32),
            jax.ShapeDtypeStruct(probe.shape, jnp.float32),
        ),
        in_specs=[pl.BlockSpec(memory_space=pltpu.SMEM)] * (1 + len(metas))
        + [far] * len(amps)
        + [whole] * (len(operands) - 1 - len(metas) - len(amps)),
        out_specs=(whole, whole),
        input_output_aliases=aliases,
        scratch_shapes=[
            pltpu.VMEM(cells_shape, jnp.float32),
            pltpu.VMEM((2, 2, size, size), jnp.float32),
            pltpu.VMEM((2, 2 * size, size), jnp.bfloat16),
            pltpu.VMEM((2, size, size), jnp.bfloat16),
            pltpu.SMEM((units + 1, 6), jnp.int32),
            pltpu.SemaphoreType.DMA((2,)),
        ],
        compiler_params=pltpu.CompilerParams(vmem_limit_bytes=32 * 1024 * 1024),
        cost_estimate=pl.CostEstimate(
            flops=units // 2 * 4 * 2 * 4 * size * size * size,
            bytes_accessed=units // 2 * 2 * size * size,
            transcendentals=units // 2 * size * size,
        ),
    )(*operands)


def joined(block):
    parts, tiles, rows, lanes = block.shape
    return block.transpose(0, 2, 1, 3).reshape(parts, rows, tiles * lanes)


def swapped(block, blk_bits=0, band_bits=0):
    groups, bands = lax.axis_size("blk"), lax.axis_size("band")
    route = [
        (g * bands + b, (g ^ blk_bits) * bands + (b ^ band_bits))
        for g in range(groups)
        for b in range(bands)
    ]
    return lax.ppermute(block, ("blk", "band"), route)


def turned(block, distance):
    groups = lax.axis_size("blk")
    return lax.ppermute(block, "blk", [(g, (g + 4 * distance) % groups) for g in range(groups)])


def to_next_band(block, blk_bits=0):
    groups, bands = lax.axis_size("blk"), lax.axis_size("band")
    route = [
        (g * bands + b, (g ^ blk_bits) * bands + b + 1)
        for g in range(groups)
        for b in range(bands - 1)
    ]
    return lax.ppermute(block, ("blk", "band"), route)


def to_previous_band(block, blk_bits=0):
    groups, bands = lax.axis_size("blk"), lax.axis_size("band")
    route = [
        (g * bands + b, (g ^ blk_bits) * bands + b - 1)
        for g in range(groups)
        for b in range(1, bands)
    ]
    return lax.ppermute(block, ("blk", "band"), route)


def summed_everywhere(block, beside):
    parts, rows, cols = block.shape
    depth = lax.axis_index("band") // 2
    sides = (
        (1, 0, lax.axis_index("blk") % 2),
        (0, 2, (depth ^ (depth // 2)) % 2),
        (0, 6, depth // 2),
    )
    block = block.reshape(parts * rows, cols)
    for blk_bits, band_bits, side in sides:
        half = block.shape[0] // 2
        kept = lax.dynamic_slice_in_dim(block, side * half, half, 0)
        sent = lax.dynamic_slice_in_dim(block, (1 - side) * half, half, 0)
        block = kept + swapped(sent, blk_bits, band_bits)
    for blk_bits, band_bits in ((4, 0), (12, 0)):
        block = block + swapped(block, blk_bits, band_bits)
    block, beside = lax.optimization_barrier((block, beside))
    for blk_bits, band_bits in ((2, 0), (2, 1)):
        block = block + swapped(block, blk_bits, band_bits)
    for blk_bits, band_bits, side in sides[::-1]:
        other = swapped(block, blk_bits, band_bits)
        block = jnp.where(
            side == 0,
            jnp.concatenate([block, other], 0),
            jnp.concatenate([other, block], 0),
        )
    return block.reshape(parts, rows, cols), beside


def near_pairs(group, slots):
    return [
        (0, 0, group, group, 0, 0, slots),
        (0, 0, group ^ 2, group ^ 2, 1, 0, slots),
        (1, 1, group, group // 2, 0, 0, slots),
        (1, 1, group ^ 2, (group ^ 2) // 2, 1, 0, slots),
    ] + [(2 + k, 2 + k, 0, 0, 1, 0, slots) for k in range(4)]


def far_pairs(group, slots):
    return [
        (0, 0, group ^ 8, group ^ 8, 0, 0, slots),
        (1, 1, group ^ 8, (group ^ 8) // 2, 0, 0, slots),
    ] + [(2, 2, source, source, 0, 0, slots) for source in range(2)]


def last_pairs(group, slots):
    return [(k, k, 0, 0, 0, 0, slots) for k in range(4)]


def body(object_band, probe, amplitudes, row_offsets, col_offsets, counts):
    size = probe.shape[1]
    rows_local = object_band.shape[1]
    slots = amplitudes.shape[3]
    bands = lax.axis_size("band")
    groups = lax.axis_size("blk")
    group = lax.axis_index("blk").astype(jnp.int32)
    line = group // 4
    lines = groups // 4
    plus, minus = dft_tables(size)
    own = amplitudes[0, 0]
    here = group[None]

    core = group % 2
    core, across = group % 2, group // 2 % 2
    paired = own.reshape(groups // 2, 2, slots, size, size)
    meta = jnp.concatenate([row_offsets[0, 0], col_offsets[0, 0], counts[0, 0][:, None]], 1)

    def units(spot, parity, source=paired):
        return lax.dynamic_slice(source, (spot, parity, 0, 0, 0), (1, 1, slots, size, size))[0]

    def notes(about, spot):
        return lax.dynamic_slice_in_dim(about, spot * 2 + core, 1, 0)

    def message(pieces, abouts):
        about = jnp.concatenate(abouts, 0)
        note = jnp.pad(about, ((0, 16 - about.shape[0]), (0, size - about.shape[1])))
        rows = [p.reshape(-1, size) for p in pieces]
        return jnp.concatenate([*rows, note.astype(jnp.bfloat16)], 0)

    def noted(received, count):
        return received[-16:, :][:count, : 2 * slots + 1].astype(jnp.int32)

    turns = (1, -1)
    ends = [(line + lines + turn) % lines * 2 for turn in turns]
    opposite = (line + 2) % lines * 2
    pieces = [message([units(e + 1 - across, core)], [notes(meta, e + 1 - across)]) for e in ends]
    rim = to_previous_band(object_band)
    early = [turned(piece, turn) for piece, turn in zip(pieces, turns)]
    main_side = swapped(object_band, 2)
    rim_side = to_previous_band(object_band, 2)
    meta_next = swapped(meta, 1)
    pieces, paired_then = lax.optimization_barrier((pieces, paired))
    theirs = swapped(lax.dynamic_index_in_dim(paired_then, 1 - core, 1, False), 1)

    def next_units(spot, source=theirs):
        return lax.dynamic_index_in_dim(source, spot, 0)

    early += [
        turned(
            message([next_units(e + 1 - across)], [notes(meta_next, e + 1 - across)]), turn
        )
        for e, turn in zip(ends, turns)
    ]
    beyond = opposite + 1 - across
    side_amps = swapped(
        message(
            [units(beyond, core), next_units(beyond)],
            [notes(meta, beyond), notes(meta_next, beyond)],
        ),
        2,
    )

    rim_then, early = lax.optimization_barrier((rim, early))
    far_board = turned(jnp.stack([object_band, rim_then]), 2)
    tile = (((0, 0), (1, 0)),)
    far_tile = (((0, 0), (0, 1)),)
    flat = own.reshape(-1, size)
    theirs_flat = theirs.reshape(-1, size)

    meta_lines = [noted(e, 1) for e in early]
    meta_side = noted(side_amps, 2)
    tables = (probe, plus, minus)

    early, paired_late, theirs_late = lax.optimization_barrier((early, paired, theirs))
    spots = [e + across for e in ends]
    late = [
        turned(message([units(spot, core, paired_late)], [notes(meta, spot)]), turn)
        for spot, turn in zip(spots, turns)
    ]
    sums, grads = cover(
        (near_pairs, slots),
        here,
        [meta, meta_next, *meta_lines],
        [flat, theirs_flat, *early],
        [object_band[None], rim[None], main_side[None], rim_side[None]],
        (((0, 0), (1, 0)), ((2, 0), (3, 0))),
        *tables,
    )
    side = sums[1].astype(jnp.bfloat16)
    side, late, theirs_late, grads = lax.optimization_barrier((side, late, theirs_late, grads))
    side = swapped(side, 2)
    late += [
        turned(message([next_units(spot, theirs_late)], [notes(meta_next, spot)]), turn)
        for spot, turn in zip(spots, turns)
    ]
    far_sums, grads = cover(
        (far_pairs, slots),
        here,
        [meta, meta_next, meta_side],
        [flat, theirs_flat, side_amps],
        [far_board],
        far_tile,
        *tables,
        None,
        grads,
    )
    far_back = far_sums[0].astype(jnp.bfloat16)
    far_back, side, grads = lax.optimization_barrier((far_back, side, grads))
    far_back = turned(far_back, 2)
    sums, grads = cover(
        (last_pairs, slots),
        here,
        [noted(e, 1) for e in late],
        late,
        [object_band[None], rim[None]],
        tile,
        *tables,
        sums,
        grads,
    )

    far_back, grads = lax.optimization_barrier((far_back, grads))
    total = sums[0] + far_back.astype(jnp.float32) + side.astype(jnp.float32)
    low = to_next_band(total[:, :, rows_local:].astype(jnp.bfloat16))
    probe_sum, low = summed_everywhere(grads, low)
    main_sums = joined(total[:, :, :rows_local] + low.astype(jnp.float32))
    probe_grad = probe_sum / groups
    power = jnp.sum(probe * probe) / (size * size)
    new_object = object_band.astype(jnp.float32) + object_rate * main_sums / (power + 1e-06)
    return (new_object, probe_grad)


def solution(mesh):
    return jax.shard_map(
        body,
        mesh=mesh,
        in_specs=(
            P(None, "band", "blk"),
            P(),
            P("blk", "band", None, None, None, None),
            P("blk", "band", None, None),
            P("blk", "band", None, None),
            P("blk", "band", None),
        ),
        out_specs=(P(None, "band", "blk"), P()),
        check_vma=False,
    )
```
